32 devices in a mesh: blk: 4 (over y, x), ctx: 8 (over z, core).
Axes of the slice: x: 2, y: 2, z: 4, core: 2. Of those that a mesh axis runs over, the one named last changes fastest.
Arguments:
- tokens: bfloat16 [4, 1024, 1024], P('blk', 'ctx'), may hold values from -16 to 16
- segment_ids: int32 [4, 1024], P('blk', 'ctx'), may hold values from 0 to 3, never falling along the last dimension, each value on 1 to 768 neighbouring positions
- norm_gain: bfloat16 [4, 2, 1024], P('blk'), may hold values from 0.25 to 1.75
- w_mamba_in: bfloat16 [4, 1024, 2048], P('blk', None, 'ctx'), may hold values from -0.1875 to 0.1875
- w_ssm_param: bfloat16 [4, 1024, 160], P('blk'), may hold values from -0.1875 to 0.1875
- ssm_rate: bfloat16 [4, 32], P('blk'), may hold values from 0.00029182434 to 0.059814453
- dt_bias: bfloat16 [4, 32], P('blk'), may hold values from -1 to 1
- skip_gain: bfloat16 [4, 32], P('blk'), may hold values from 0.5 to 1.5
- ssm_norm_gain: bfloat16 [4, 2048], P('blk'), may hold values from 0.25 to 1.75
- w_mamba_out: bfloat16 [4, 2048, 1024], P('blk', 'ctx'), may hold values from -0.125 to 0.125
- w_qkv: bfloat16 [4, 1024, 2048], P('blk', None, 'ctx'), may hold values from -1.5 to 1.5
- w_attn_out: bfloat16 [4, 1024, 1024], P('blk', 'ctx'), may hold values from -0.75 to 0.75
Outputs:
- layer_out: bfloat16 [4, 1024, 1024], P('blk', 'ctx')
The draws below stay inside these ranges and needn't reach their ends.
Inputs may be any that keep to these rules, and one draw needn't show every extreme that they name: `segment_ids`: within each micro-batch the ids never fall along the sequence; each document holds 1 to 768 tokens, and one holds exactly that many.
All inputs are finite; a program needn't handle non-finite values.
Results may differ from the reference program's by a relative error of at most 0.015.
Values may be sent and summed in bfloat16 or wider, within the bound.
A program may use at most 128 MiB of HBM per device.

```python
import math
import jax
import jax.numpy as jnp
import numpy as np
from jax import lax

MODEL = 1024
INNER = 2048
HEAD_DIM = 64
STATE = 64
QUERY_HEADS = 8
KV_HEADS = 4
ATTN_DIM = 128
SPAN = 64
SSM_HEADS = 32
SECTIONS = 4
LENGTH = 1024


def draw_tokens(key, part):
    base = jax.random.normal(jax.random.fold_in(key, 7011), (SECTIONS, LENGTH, MODEL), jnp.float32)
    return jnp.clip(base, -6.0, 6.0).astype(jnp.bfloat16)


def draw_w_qkv(key, part):
    columns = (QUERY_HEADS + 2 * KV_HEADS) * ATTN_DIM
    base = jax.random.normal(jax.random.fold_in(key, 7021), (SECTIONS, MODEL, columns), jnp.float32) / math.sqrt(MODEL)
    return jnp.clip(base, -1.5, 1.5).astype(jnp.bfloat16)


def block_scale(key, extent, pieces, smallest, high):
    def one(dim, parts):
        steps = jax.random.uniform(jax.random.fold_in(jax.random.fold_in(key, 6), dim), (parts,), jnp.float32, smallest / len(pieces), high / len(pieces))
        return jnp.repeat(jnp.exp(steps), extent[dim] // parts).reshape((-1,) + (1,) * (len(extent) - dim - 1))

    level = one(*pieces[0])
    for cut in pieces[1:]:
        level = level * one(*cut)
    return level


def length_profile(amount, total, most, slope):
    weights = [(1 << 20) // math.isqrt(grade ** slope) + 1 for grade in range(2, amount + 1)]
    spare, holding = total - most - (amount - 1), [1] * (amount - 1)
    while spare > 0:
        candidates = [i for i in range(amount - 1) if holding[i] < most]
        whole, budget = sum([weights[i] for i in candidates]), spare
        for i in candidates:
            extra = min(most - holding[i], max(1, budget * weights[i] // whole), spare)
            holding[i] = holding[i] + extra
            spare = spare - extra
    return np.array([most] + holding)


def uneven(key, count, total, bound, lean):
    if count == 2:
        one = jax.random.randint(key, (), max(1, total - bound), min(bound, total - 1) + 1)
        return jnp.stack([one, total - one])
    tallies = jnp.asarray(length_profile(count, total, bound, lean), jnp.int32)
    pairs = (count - 1) // 2
    giver, taker = tallies[1:1 + 2 * pairs:2], tallies[2:2 + 2 * pairs:2]
    room = jnp.minimum(giver - 1, bound - taker)
    shifted = jax.random.randint(jax.random.fold_in(key, 1), (pairs,), 0, 1 << 20) % (room + 1)
    tallies = tallies.at[1:1 + 2 * pairs:2].set(giver - shifted).at[2:2 + 2 * pairs:2].set(taker + shifted)
    return tallies[jax.random.permutation(jax.random.fold_in(key, 2), count)]


def noise(own_key, dims, deviation, limit, split=(), kind=jnp.bfloat16):
    values = jax.random.normal(own_key, dims, jnp.float32) * deviation
    if len(split) > 0:
        values = block_scale(own_key, dims, split, -0.22, 0.18) * values
    return jnp.clip(values, min=-limit, max=limit).astype(kind)


def setup_inputs(seed: int = 0) -> dict:
    key_of = jax.random.split(jax.random.key(seed), 13)
    return {
        "tokens": draw_tokens(jax.random.fold_in(key_of[12], 71), 0),
        "segment_ids": jax.vmap(lambda own: jnp.searchsorted(jnp.cumsum(uneven(own, 4, LENGTH, 3 * LENGTH // 4, 1)), jnp.arange(LENGTH), side="right"))(jax.random.split(key_of[1], SECTIONS)).reshape((SECTIONS, LENGTH)).astype(jnp.int32),
        "norm_gain": jnp.clip(1.0 + 0.15 * jax.random.normal(key_of[2], (SECTIONS, 2, MODEL), jnp.float32), 0.25, 1.75).astype(jnp.bfloat16),
        "w_mamba_in": noise(key_of[3], (SECTIONS, MODEL, INNER), MODEL ** -0.5, 0.1875, ((0, 4), (2, 8))),
        "w_ssm_param": noise(key_of[4], (SECTIONS, MODEL, 2 * STATE + SSM_HEADS), MODEL ** -0.5, 0.1875, ((0, 4),)),
        "ssm_rate": jnp.clip(jnp.exp(math.log(0.059814453) - 5.3228506 * jax.random.uniform(key_of[5], (SECTIONS, SSM_HEADS), jnp.float32) ** block_scale(key_of[5], (SECTIONS, SSM_HEADS), ((0, 4),), -0.2, 0.2)), 0.00029182434, 0.059814453).astype(jnp.bfloat16),
        "dt_bias": jnp.clip(jax.random.uniform(key_of[6], (SECTIONS, SSM_HEADS), jnp.float32, -1.0, 1.0) * block_scale(key_of[6], (SECTIONS, SSM_HEADS), ((0, 4),), -0.4, 0.0), -1.0, 1.0).astype(jnp.bfloat16),
        "skip_gain": jnp.clip(0.5 + 1.0 * jax.random.uniform(key_of[7], (SECTIONS, SSM_HEADS), jnp.float32) ** block_scale(key_of[7], (SECTIONS, SSM_HEADS), ((0, 4),), -0.2, 0.2), 0.5, 1.5).astype(jnp.bfloat16),
        "ssm_norm_gain": jnp.clip(1.0 + 0.15 * jax.random.normal(key_of[8], (SECTIONS, INNER), jnp.float32), 0.25, 1.75).astype(jnp.bfloat16),
        "w_mamba_out": noise(key_of[9], (SECTIONS, INNER, MODEL), INNER ** -0.5, 0.125, ((0, 4), (1, 8))),
        "w_qkv": draw_w_qkv(jax.random.fold_in(key_of[12], 71), 0),
        "w_attn_out": noise(key_of[11], (SECTIONS, QUERY_HEADS * ATTN_DIM, MODEL), (QUERY_HEADS * ATTN_DIM // 16) ** -0.5, 0.75, ((0, 4), (1, 8))),
    }


epsilon = 1e-05
highest = lax.Precision.HIGHEST

def rms_norm(values, gain):
    values = values.astype(jnp.float32)
    scale = lax.rsqrt(lax.optimization_barrier(jnp.mean(values * values, axis=-1, keepdims=True)) + epsilon)
    return values * scale * gain.astype(jnp.float32)

def span_update(carry, block):
    state, prev_segment = carry
    inner_value, bin_value, cout_value, delta, log_decay, segment = block
    cumul = jnp.cumsum(log_decay, axis=0)
    order = jnp.arange(segment.shape[0])
    allowed = (order[:, None] >= order[None, :]) & (segment[:, None] == segment[None, :])
    differ = cumul[:, None, :] - cumul[None, :, :]
    factor = jnp.where(allowed[:, :, None], jnp.exp(jnp.minimum(differ, 0.0)), 0.0)
    intersection = jnp.dot(cout_value, bin_value.T, precision=highest)
    mixing = factor * intersection[:, :, None] * delta[None, :, :]
    within = jnp.einsum('tsh,shp->thp', mixing, inner_value, precision=highest)
    carried = jnp.where((segment == prev_segment)[:, None], jnp.exp(cumul), 0.0)
    across = jnp.einsum('tn,hpn->thp', cout_value, state, precision=highest) * carried[:, :, None]
    last_segment = segment[-1]
    keeping = jnp.where((segment == last_segment)[:, None], jnp.exp(cumul[-1][None, :] - cumul), 0.0) * delta
    fresh = jnp.einsum('sh,shp,sn->hpn', keeping, inner_value, bin_value, precision=highest)
    passing = jnp.where(prev_segment == last_segment, jnp.exp(cumul[-1]), 0.0)
    state = passing[:, None, None] * state + fresh
    return ((state, last_segment), within + across)

def micro_batch(tokens, segment, norm_gain, w_mamba_in, w_ssm_param, ssm_rate, dt_bias, skip_gain, ssm_norm_gain, w_mamba_out, w_qkv, w_attn_out):
    length = tokens.shape[0]
    heads = SSM_HEADS
    normed = rms_norm(tokens, norm_gain[0]).astype(jnp.bfloat16)
    inner = jnp.dot(normed, w_mamba_in, preferred_element_type=jnp.float32).astype(jnp.bfloat16)
    params = jnp.dot(normed, w_ssm_param, preferred_element_type=jnp.float32)
    bin_value = params[:, :STATE]
    cout_value = params[:, STATE:2 * STATE]
    delta = jax.nn.softplus(params[:, 2 * STATE:] + dt_bias.astype(jnp.float32))
    log_decay = -delta * ssm_rate.astype(jnp.float32)
    inner_value = inner.astype(jnp.float32).reshape(length, heads, HEAD_DIM)
    blocks = tuple((item.reshape((length // SPAN, SPAN) + item.shape[1:]) for item in (inner_value, bin_value, cout_value, delta, log_decay, segment)))
    start_carry = (jnp.zeros((heads, HEAD_DIM, STATE), jnp.float32), jnp.array(-1, jnp.int32))
    ignored, mixed = lax.scan(span_update, start_carry, blocks)
    mixed = mixed.reshape(length, heads, HEAD_DIM) + skip_gain.astype(jnp.float32)[None, :, None] * inner_value
    ssm_out = rms_norm(mixed.reshape(length, INNER), ssm_norm_gain).astype(jnp.bfloat16)
    first = tokens.astype(jnp.float32) + jnp.dot(ssm_out, w_mamba_out, preferred_element_type=jnp.float32)
    hidden = rms_norm(first, norm_gain[1]).astype(jnp.bfloat16)
    projected = jnp.dot(hidden, w_qkv, preferred_element_type=jnp.float32).astype(jnp.bfloat16)
    groups = QUERY_HEADS // KV_HEADS
    query = projected[:, :QUERY_HEADS * ATTN_DIM].reshape(length, KV_HEADS, groups, ATTN_DIM).astype(jnp.float32)
    keys = projected[:, QUERY_HEADS * ATTN_DIM:(QUERY_HEADS + KV_HEADS) * ATTN_DIM].reshape(length, KV_HEADS, ATTN_DIM).astype(jnp.float32)
    values = projected[:, (QUERY_HEADS + KV_HEADS) * ATTN_DIM:].reshape(length, KV_HEADS, ATTN_DIM).astype(jnp.float32)
    positions = jnp.arange(length)
    width = math.gcd(512, length)
    scale = 1.0 / math.sqrt(ATTN_DIM)

    def attend(block_index):
        begin = block_index * width
        query_block = lax.dynamic_slice_in_dim(query, begin, width, 0)
        query_segment = lax.dynamic_slice_in_dim(segment, begin, width, 0)
        query_position = begin + jnp.arange(width)
        scores = jnp.einsum('tkgd,skd->kgts', query_block, keys, precision=highest) * scale
        allowed = (positions[None, :] <= query_position[:, None]) & (segment[None, :] == query_segment[:, None])
        scores = jnp.where(allowed, scores, -1e+30)
        top = lax.optimization_barrier(jnp.max(scores, axis=-1, keepdims=True))
        probs = jnp.where(allowed, jnp.exp(scores - top), 0.0)
        total = lax.optimization_barrier(jnp.sum(probs, axis=-1))
        rounded = probs.astype(jnp.bfloat16).astype(jnp.float32)
        context = jnp.einsum('kgts,skd->kgtd', rounded, values, precision=highest) / total[..., None]
        return jnp.transpose(context, (2, 0, 1, 3)).reshape(width, QUERY_HEADS * ATTN_DIM).astype(jnp.bfloat16)
    context = lax.map(attend, jnp.arange(length // width)).reshape(length, QUERY_HEADS * ATTN_DIM)
    result = first + jnp.dot(context, w_attn_out, preferred_element_type=jnp.float32)
    return result.astype(jnp.bfloat16)

def reference(tokens, segment_ids, norm_gain, w_mamba_in, w_ssm_param, ssm_rate, dt_bias, skip_gain, ssm_norm_gain, w_mamba_out, w_qkv, w_attn_out):
    weights = (norm_gain, w_mamba_in, w_ssm_param, ssm_rate, dt_bias, skip_gain, ssm_norm_gain, w_mamba_out, w_qkv, w_attn_out)
    rolled = tuple((jnp.roll(item, 1, axis=0) for item in weights))
    outputs = []
    for batch_index in range(tokens.shape[0]):
        section = tuple((item[batch_index] for item in rolled))
        outputs.append(micro_batch(tokens[batch_index], segment_ids[batch_index], section[0], section[1], section[2], section[3], section[4], section[5], section[6], section[7], section[8], section[9]))
    return jnp.stack(outputs, axis=0)
```

```python
import functools
import math

import jax
import jax.numpy as jnp
from jax import lax
from jax.experimental import pallas as pl
from jax.experimental.pallas import tpu as pltpu
from jax.sharding import PartitionSpec as P

INNER = 2048
HEAD_DIM = 64
STATE = 64
QUERY_HEADS = 8
KV_HEADS = 4
ATTN_DIM = 128
SPAN = 64


epsilon = 1e-05
highest = lax.Precision.HIGHEST


def prefix(value, axis, join, neutral):
    count, mine = (lax.axis_size(axis), lax.axis_index(axis))
    pieces = jax.tree.map(lambda part: lax.all_gather(part, axis), value)
    so_far = jax.tree.map(
        lambda part, zero: jnp.full_like(part, 0) + jnp.asarray(zero, part.dtype), value, neutral
    )

    def hop(position, so_far):
        longer = join(so_far, jax.tree.map(lambda part: part[position], pieces))
        return jax.tree.map(lambda new, old: jnp.where(position < mine, new, old), longer, so_far)

    return lax.fori_loop(0, count - 1, hop, so_far)


def from_behind(value, axis, steps):
    count = lax.axis_size(axis)
    pairs = [(source, (source + steps) % count) for source in range(count)]
    return lax.ppermute(value, axis, pairs)


def rms_norm(values, gain):
    values = values.astype(jnp.float32)
    scale = lax.rsqrt(jnp.mean(values * values, axis=-1, keepdims=True) + epsilon)
    return values * scale * gain.astype(jnp.float32)


def running_sum(values):
    count = values.shape[0]
    lower = jnp.tril(jnp.ones((count, count), jnp.float32))
    return jnp.dot(lower, values, precision=highest)


def span_update(carry, block):
    state, prev_segment = carry
    inner_value, bin_value, cout_value, delta, log_decay, segment = block
    cumul = running_sum(log_decay)
    order = jnp.arange(segment.shape[0])
    allowed = (order[:, None] >= order[None, :]) & (segment[:, None] == segment[None, :])
    differ = cumul[:, None, :] - cumul[None, :, :]
    factor = jnp.where(allowed[:, :, None], jnp.exp(jnp.minimum(differ, 0.0)), 0.0)
    intersection = jnp.dot(cout_value, bin_value.T, precision=highest)
    mixing = factor * intersection[:, :, None] * delta[None, :, :]
    within = jnp.einsum("tsh,shp->thp", mixing, inner_value, precision=highest)
    carried = jnp.where((segment == prev_segment)[:, None], jnp.exp(cumul), 0.0)
    across = jnp.einsum("tn,hpn->thp", cout_value, state, precision=highest) * carried[:, :, None]
    last_segment = segment[-1]
    keeping = (
        jnp.where((segment == last_segment)[:, None], jnp.exp(cumul[-1][None, :] - cumul), 0.0)
        * delta
    )
    fresh = jnp.einsum("sh,shp,sn->hpn", keeping, inner_value, bin_value, precision=highest)
    passing = jnp.where(prev_segment == last_segment, jnp.exp(cumul[-1]), 0.0)
    state = passing[:, None, None] * state + fresh
    return ((state, last_segment), within + across)


def combine_states(earlier, later):
    early_first, early_last, early_pass, early_state = earlier
    late_first, late_last, late_pass, late_state = later
    joined = (late_first == early_last) | (early_last < 0) | (late_first < 0)
    factor = jnp.where(joined, late_pass, 0.0)
    first = jnp.where(early_first < 0, late_first, early_first)
    last = jnp.where(late_last < 0, early_last, late_last)
    return (first, last, early_pass * factor, factor[:, None, None] * early_state + late_state)


def layer_pair(tokens, segment, weights):
    (
        norm_gain,
        w_mamba_in,
        w_ssm_param,
        ssm_rate,
        dt_bias,
        skip_gain,
        ssm_norm_gain,
        w_mamba_out,
        w_qkv,
        w_attn_out,
    ) = weights
    rows = tokens.shape[0]
    heads = ssm_rate.shape[0]
    offset = lax.axis_index("ctx") * rows
    normed = rms_norm(tokens, norm_gain[0]).astype(jnp.bfloat16)
    slab = jnp.dot(
        lax.all_gather(normed, "ctx", axis=0, tiled=True),
        w_mamba_in,
        preferred_element_type=jnp.float32,
    ).astype(jnp.bfloat16)
    inner = lax.all_to_all(slab, "ctx", split_axis=0, concat_axis=1, tiled=True)
    params = jnp.dot(normed, w_ssm_param, preferred_element_type=jnp.float32)
    bin_value = params[:, :STATE]
    cout_value = params[:, STATE : 2 * STATE]
    delta = jax.nn.softplus(params[:, 2 * STATE :] + dt_bias.astype(jnp.float32))
    log_decay = -delta * ssm_rate.astype(jnp.float32)
    inner_value = inner.astype(jnp.float32).reshape(rows, heads, HEAD_DIM)
    blocks = tuple(
        (
            item.reshape((rows // SPAN, SPAN) + item.shape[1:])
            for item in (inner_value, bin_value, cout_value, delta, log_decay, segment)
        )
    )
    start_carry = (jnp.zeros((heads, HEAD_DIM, STATE), jnp.float32), segment[0])
    (local_state, ignored), mixed = lax.scan(span_update, start_carry, blocks)
    device_decay = running_sum(log_decay)
    through = jnp.where(segment[0] == segment[-1], jnp.exp(device_decay[-1]), 0.0)
    element = (segment[0], segment[-1], through, local_state)
    identity = (
        jnp.array(-1, jnp.int32),
        jnp.array(-1, jnp.int32),
        jnp.ones_like(through),
        jnp.zeros_like(local_state),
    )
    scanned = prefix(element, "ctx", combine_states, identity)
    incoming_segment = scanned[1]
    incoming_state = scanned[3]
    linked = jnp.where((segment == incoming_segment)[:, None], jnp.exp(device_decay), 0.0)
    entering = (
        jnp.einsum("tn,hpn->thp", cout_value, incoming_state, precision=highest)
        * linked[:, :, None]
    )
    mixed = (
        mixed.reshape(rows, heads, HEAD_DIM)
        + entering
        + skip_gain.astype(jnp.float32)[None, :, None] * inner_value
    )
    ssm_out = rms_norm(mixed.reshape(rows, INNER), ssm_norm_gain).astype(jnp.bfloat16)
    columns = ssm_out
    first = tokens.astype(jnp.float32) + jnp.dot(
        columns,
        lax.all_gather(w_mamba_out, "ctx", axis=0, tiled=True),
        preferred_element_type=jnp.float32,
    )
    hidden = rms_norm(first, norm_gain[1]).astype(jnp.bfloat16)
    projected = jnp.dot(
        hidden, lax.all_gather(w_qkv, "ctx", axis=1, tiled=True), preferred_element_type=jnp.float32
    ).astype(jnp.bfloat16)
    groups = QUERY_HEADS // KV_HEADS
    query = projected[:, : QUERY_HEADS * ATTN_DIM].reshape(rows, KV_HEADS, groups, ATTN_DIM)
    keys = projected[:, QUERY_HEADS * ATTN_DIM : (QUERY_HEADS + KV_HEADS) * ATTN_DIM]
    values = projected[:, (QUERY_HEADS + KV_HEADS) * ATTN_DIM :]
    positions = offset + jnp.arange(rows)
    scale = 1.0 / math.sqrt(ATTN_DIM)
    top = jnp.full((KV_HEADS, groups, rows), -1e30, jnp.float32)
    key_piece = lax.all_gather(keys, "ctx", axis=0, tiled=True)
    value_piece = lax.all_gather(values, "ctx", axis=0, tiled=True)
    segment_piece = lax.all_gather(segment, "ctx", axis=0, tiled=True)
    count = key_piece.shape[0]
    key_position = jnp.arange(count)
    scores = (
        jnp.einsum(
            "tkgd,skd->kgts",
            query,
            key_piece.reshape(count, KV_HEADS, ATTN_DIM),
            preferred_element_type=jnp.float32,
        )
        * scale
    )
    allowed = (key_position[None, :] <= positions[:, None]) & (
        segment_piece[None, :] == segment[:, None]
    )
    scores = jnp.where(allowed, scores, -1e30)
    new_top = jnp.maximum(top, jnp.max(scores, axis=-1))
    probs = jnp.where(allowed, jnp.exp(scores - new_top[..., None]), 0.0)
    total = jnp.sum(probs, axis=-1)
    attend_context = jnp.einsum(
        "kgts,skd->kgtd",
        probs.astype(jnp.bfloat16),
        value_piece.reshape(count, KV_HEADS, ATTN_DIM),
        preferred_element_type=jnp.float32,
    )
    top, total, context = (new_top, total, attend_context)
    context = context / total[..., None]
    context = (
        jnp.transpose(context, (2, 0, 1, 3))
        .reshape(rows, QUERY_HEADS * ATTN_DIM)
        .astype(jnp.bfloat16)
    )
    columns = context
    result = first + jnp.dot(
        columns,
        lax.all_gather(w_attn_out, "ctx", axis=0, tiled=True),
        preferred_element_type=jnp.float32,
    )
    return result.astype(jnp.bfloat16)


MESH = pl.DeviceIdType.MESH
float32, bfloat16 = jnp.float32, jnp.bfloat16


def fits_fused(tokens, w_qkv):
    count = lax.axis_size("ctx")
    return (
        lax.axis_size("blk") > 1
        and count == QUERY_HEADS
        and QUERY_HEADS == 2 * KV_HEADS
        and tokens.shape[1] % 128 == 0
        and w_qkv.shape[2] % ATTN_DIM == 0
    )


def remote(source, target, send_sem, recv_sem, blk, ctx):
    return pltpu.make_async_remote_copy(
        src_ref=source,
        dst_ref=target,
        send_sem=send_sem,
        recv_sem=recv_sem,
        device_id=(blk, ctx),
        device_id_type=MESH,
    )


def dot(a, b, contract=((1,), (0,)), precision=None):
    return lax.dot_general(
        a, b, (contract, ((), ())), precision=precision, preferred_element_type=float32
    )


def to_column(row, rows):
    return jnp.broadcast_to(row, (rows, rows)).T


def fused_kernel(
    tok_ref,
    seg_ref,
    gain_ref,
    win_ref,
    wssm_ref,
    small_ref,
    sgain_ref,
    wout_ref,
    wqkv_ref,
    wao_ref,
    out_ref,
    xbuf,
    segbuf,
    segcol,
    segrow,
    prev_ref,
    state_ref,
    nall,
    hall,
    mix_ref,
    ctx_ref,
    wbuf,
    qbuf,
    kbuf,
    vbuf,
    own_ref,
    first_ref,
    sqsend,
    sqbuf,
    pairsend,
    pairbuf,
    rssend,
    rsbuf,
    hop_sem,
    seg_send,
    seg_recv,
    ag_send,
    ag_fwd,
    ag_recv,
    w_send,
    w_fwd,
    w_recv,
    sq_send,
    sq_recv,
    pair_send,
    pair_recv,
    rs_send,
    rs_recv,
):
    n, nb = lax.axis_size("ctx"), lax.axis_size("blk")
    chips = n // 2
    me, blk = lax.axis_index("ctx"), lax.axis_index("blk")
    chip, core = me // 2, me % 2
    sibling = chip * 2 + 1 - core
    ahead, behind = (blk + 1) % nb, (blk + nb - 1) % nb
    rows, model = tok_ref.shape
    length = n * rows
    wide = 2 * rows
    width = win_ref.shape[1]
    heads = small_ref.shape[1]
    mine = width // HEAD_DIM
    inner_total = sgain_ref.shape[1]
    held = wqkv_ref.shape[1] // ATTN_DIM

    barrier = pltpu.get_barrier_semaphore()
    for k in range(1, n):
        pl.semaphore_signal(barrier, inc=1, device_id=(blk, (me + k) % n), device_id_type=MESH)
    for other in (ahead, behind):
        pl.semaphore_signal(barrier, inc=1, device_id=(other, me), device_id_type=MESH)
    pl.semaphore_wait(barrier, n + 1)

    hop = remote(tok_ref, xbuf, hop_sem.at[0], hop_sem.at[1], behind, me)
    hop.start()
    seg_hop = remote(seg_ref, segbuf.at[me], hop_sem.at[2], seg_recv.at[me], behind, me)
    seg_hop.start()

    plan = []
    for e in range(n):
        plan.append((0, e, e))
    for j in range(KV_HEADS):
        plan.append((1, QUERY_HEADS + j, 2 * j))
        plan.append((2, QUERY_HEADS + KV_HEADS + j, 2 * j + 1))

    def weight_copy(kind, head, target):
        part = wqkv_ref.at[:, pl.ds((head % held) * ATTN_DIM, ATTN_DIM)]
        return remote(part, wbuf.at[kind], w_send.at[kind, target], w_recv.at[kind], blk, target)

    for kind, head, target in plan:

        @pl.when(me == head // held)
        def _():
            if head // held == target:
                wbuf[kind] = wqkv_ref[:, (head % held) * ATTN_DIM : (head % held + 1) * ATTN_DIM]
            else:
                weight_copy(kind, head, target).start()

    def weight_wait(kind):
        remote(wbuf.at[0], wbuf.at[kind], w_send.at[0, 0], w_recv.at[kind], blk, sibling).wait_recv()

    def not_own(kind, then):
        own = [t for k, h, t in plan if k == kind and h // held == t]
        here = me >= 0
        for target in own:
            here = here & (me != target)
        pl.when(here)(then)

    def gather_start(buf, stage):
        sends = []
        for k in range(chips):
            target = sibling if k == 0 else ((chip + k) % chips) * 2 + core
            copy = remote(
                buf.at[me], buf.at[me], ag_send.at[stage, k], ag_recv.at[stage, me], blk, target
            )
            copy.start()
            sends.append(copy)
        return sends

    def gather_wait(buf, stage, source):
        remote(
            buf.at[source],
            buf.at[source],
            ag_send.at[stage, 0],
            ag_recv.at[stage, source],
            blk,
            sibling,
        ).wait_recv()

    def forward(buf, stage, p):
        source = 2 * p + core
        return remote(
            buf.at[source],
            buf.at[source],
            ag_fwd.at[stage, p],
            ag_recv.at[stage, source],
            blk,
            sibling,
        )

    def gather_step(buf, stage, p):
        @pl.when(p != chip)
        def _():
            gather_wait(buf, stage, 2 * p + core)
            forward(buf, stage, p).start()

        gather_wait(buf, stage, 2 * p + 1 - core)

    def pair_copy(stage, p):
        return remote(
            pairsend.at[stage, p],
            pairbuf.at[stage, p],
            pair_send.at[stage, p],
            pair_recv.at[stage, p],
            blk,
            sibling,
        )

    def rs_copy(stage, p, source):
        return remote(
            rssend.at[stage, p],
            rsbuf.at[stage, source],
            rs_send.at[stage, p],
            rs_recv.at[stage, source],
            blk,
            2 * p + core,
        )

    def scatter_step(stage, p, left, weight_ref):
        pairsend[stage, p] = dot(left[1 - core], weight_ref[...]).astype(bfloat16)
        pair_copy(stage, p).start()
        part = dot(left[core], weight_ref[...])
        pair_copy(stage, p).wait_recv()
        part = part + pairbuf[stage, p].astype(float32)

        @pl.when(p == chip)
        def _():
            own_ref[...] = part

        @pl.when(p != chip)
        def _():
            rssend[stage, p] = part.astype(bfloat16)
            rs_copy(stage, p, chip).start()

    def scatter_end(stage):
        total = own_ref[...]
        for k in range(1, chips):
            source = (chip + k) % chips
            rs_copy(stage, source, source).wait_recv()
            total = total + rsbuf[stage, source].astype(float32)
        return total

    def sq_copy(target, source):
        return remote(
            sqsend.at[target], sqbuf.at[source], sq_send.at[target], sq_recv.at[source], blk, target
        )

    hop.wait_recv()
    x = xbuf[...].astype(float32)
    scale = lax.rsqrt(jnp.mean(x * x, axis=-1, keepdims=True) + epsilon)
    nall[me] = (x * scale * gain_ref[0:1, :].astype(float32)).astype(bfloat16)
    sends = gather_start(nall, 0)
    seg_hop_in = remote(seg_ref, segbuf.at[me], hop_sem.at[2], seg_recv.at[me], behind, me)
    seg_hop_in.wait_recv()
    for k in range(1, n):
        copy = remote(
            segbuf.at[me], segbuf.at[me], seg_send.at[k], seg_recv.at[me], blk, (me + k) % n
        )
        copy.start()
        sends.append(copy)
    for k in range(1, n):
        source = (me + k) % n
        remote(
            segbuf.at[source], segbuf.at[source], seg_send.at[k], seg_recv.at[source], blk, source
        ).wait_recv()
    for j in range(n):
        segrow[:, j * rows : (j + 1) * rows] = segbuf[j]
        segcol[j * rows : (j + 1) * rows, :] = to_column(segbuf[j][0:1, :], rows)
    prev_ref[...] = segbuf[0]
    state_ref[...] = jnp.zeros_like(state_ref)

    head_row = lax.broadcasted_iota(jnp.int32, (heads, 128), 0)
    head_lane = lax.broadcasted_iota(jnp.int32, (heads, 128), 1)
    pick = (head_row == head_lane + me * mine).astype(float32)
    pick = jnp.where(head_lane < mine, pick, 0.0)
    wide_row = lax.broadcasted_iota(jnp.int32, (heads, width), 0)
    wide_lane = lax.broadcasted_iota(jnp.int32, (heads, width), 1)
    spread = (wide_row == wide_lane // HEAD_DIM + me * mine).astype(float32)
    lane_head = lax.broadcasted_iota(jnp.int32, (wide, width), 1) // HEAD_DIM
    later = lax.broadcasted_iota(jnp.int32, (wide, wide), 0)
    earlier = lax.broadcasted_iota(jnp.int32, (wide, wide), 1)
    lower = (later >= earlier).astype(float32)
    rate, bias = small_ref[0:1, :], small_ref[1:2, :]
    skip = dot(small_ref[...], spread, precision=highest)[2:3, :]
    sgain = sgain_ref[:, pl.ds(pl.multiple_of(me * width, width), width)].astype(float32)

    def mamba_step(p, carry):
        gather_step(nall, 0, p)
        block = nall[pl.ds(2 * p, 2)].reshape(wide, model)
        u = dot(block, win_ref[...]).astype(bfloat16).astype(float32)
        params = dot(block, wssm_ref[...])
        bin_value = params[:, :STATE].astype(bfloat16)
        cout_value = params[:, STATE : 2 * STATE].astype(bfloat16)
        raw = params[:, 2 * STATE :] + bias
        delta = jnp.maximum(raw, 0.0) + jnp.log1p(jnp.exp(-jnp.abs(raw)))
        cumul = dot(lower, -delta * rate, precision=highest)
        cumul_column = dot(cumul, pick, precision=highest)
        cumul_row = cumul_column.T
        cumul_wide = dot(cumul, spread, precision=highest)
        fed = dot(delta, spread, precision=highest) * u
        fed_short = fed.astype(bfloat16)
        begin = pl.multiple_of(p * wide, wide)
        seg_column = segcol[pl.ds(begin, wide), 0:1]
        seg_row = segrow[0:1, pl.ds(begin, wide)]
        prev = prev_ref[0:1, 0:1]
        last = seg_row[0:1, wide - 1 : wide]
        allowed = (seg_column == seg_row) & (later >= earlier)
        crossing = dot(cout_value, bin_value, ((1,), (1,)))
        mixed = jnp.zeros((wide, width), float32)
        for h in range(mine):
            differ = cumul_column[:, h : h + 1] - cumul_row[h : h + 1, :]
            factor = jnp.where(allowed, jnp.exp(jnp.minimum(differ, 0.0)) * crossing, 0.0)
            mixed = jnp.where(lane_head == h, dot(factor.astype(bfloat16), fed_short), mixed)
        state = state_ref[...]
        mixed = mixed + dot(cout_value, state.astype(bfloat16)) * jnp.where(
            seg_column == prev, jnp.exp(cumul_wide), 0.0
        )
        mixed = mixed + skip * u
        final = cumul_wide[wide - 1 : wide, :]
        keep = jnp.where(seg_column == last, jnp.exp(final - cumul_wide), 0.0)
        fresh = dot(bin_value, (keep * fed).astype(bfloat16), ((0,), (0,)))
        state_ref[...] = jnp.where(prev == last, jnp.exp(final), 0.0) * state + fresh
        prev_ref[...] = jnp.broadcast_to(last, prev_ref.shape)
        square = jnp.sum(mixed * mixed, axis=-1, keepdims=True)
        mixed = (mixed * sgain).astype(bfloat16)
        for o in range(2):
            mix_ref[o] = mixed[o * rows : (o + 1) * rows]
            flat = jnp.broadcast_to(square[o * rows : (o + 1) * rows], (rows, rows)).T[:8]
            target = 2 * p + o

            @pl.when(target == me)
            def _():
                sqbuf[me] = flat

            @pl.when(target != me)
            def _():
                sqsend[target] = flat
                sq_copy(target, me).start()

        scatter_step(0, p, mix_ref, wout_ref)
        return carry

    lax.fori_loop(0, chips, mamba_step, 0)

    not_own(1, lambda: pl.when(core == 0)(lambda: weight_wait(1)))
    not_own(2, lambda: pl.when(core == 1)(lambda: weight_wait(2)))
    passed = remote(
        wbuf.at[1 + core], wbuf.at[1 + core], w_fwd.at[0], w_recv.at[1 + core], blk, sibling
    )
    passed.start()
    sends.append(passed)

    total = scatter_end(0)
    for k in range(1, n):
        source = (me + k) % n
        sq_copy(source, source).wait_recv()
    squares = sqbuf[0]
    for j in range(1, n):
        squares = squares + sqbuf[j]
    squares = to_column(squares[0:1, :], rows)[:, 0:1]
    first = xbuf[...].astype(float32) + total * lax.rsqrt(squares / inner_total + epsilon)
    first_ref[...] = first
    scale = lax.rsqrt(jnp.mean(first * first, axis=-1, keepdims=True) + epsilon)
    hall[me] = (first * scale * gain_ref[1:2, :].astype(float32)).astype(bfloat16)
    sends += gather_start(hall, 1)

    not_own(0, lambda: weight_wait(0))
    weight_wait(2 - core)
    for p in range(chips):
        gather_step(hall, 1, p)
        block = hall[pl.ds(2 * p, 2)].reshape(wide, model)
        here = slice(p * wide, (p + 1) * wide)
        upto = (p + 1) * wide
        query = dot(block, wbuf[0]).astype(bfloat16)
        kbuf[here, :] = dot(block, wbuf[1]).astype(bfloat16)
        vbuf[here, :] = dot(block, wbuf[2]).astype(bfloat16)
        scores = dot(query, kbuf[:upto, :], ((1,), (1,))) * (1.0 / math.sqrt(ATTN_DIM))
        at = p * wide + lax.broadcasted_iota(jnp.int32, (wide, upto), 0)
        key_at = lax.broadcasted_iota(jnp.int32, (wide, upto), 1)
        allowed = (key_at <= at) & (segcol[here, 0:1] == segrow[0:1, :upto])
        scores = jnp.where(allowed, scores, -1e30)
        top = jnp.max(scores, axis=-1, keepdims=True)
        probs = jnp.where(allowed, jnp.exp(scores - top), 0.0)
        weight = jnp.sum(probs, axis=-1, keepdims=True)
        context = (dot(probs.astype(bfloat16), vbuf[:upto, :]) / weight).astype(bfloat16)
        for o in range(2):
            ctx_ref[o] = context[o * rows : (o + 1) * rows]
        scatter_step(1, p, ctx_ref, wao_ref)

    result = first_ref[...] + scatter_end(1)
    qbuf[...] = result.astype(bfloat16)
    back = remote(qbuf, out_ref, hop_sem.at[3], hop_sem.at[4], ahead, me)
    back.start()

    for copy in sends:
        copy.wait_send()
    hop.wait_send()
    seg_hop.wait_send()
    for kind, head, target in plan:
        if head // held != target:

            @pl.when(me == head // held)
            def _():
                weight_copy(kind, head, target).wait_send()

    for j in range(n):

        @pl.when(me != j)
        def _():
            sq_copy(j, me).wait_send()

    for p in range(chips):
        for stage, buf in ((0, nall), (1, hall)):
            pair_copy(stage, p).wait_send()

            @pl.when(chip != p)
            def _():
                forward(buf, stage, p).wait_send()
                rs_copy(stage, p, chip).wait_send()

    back.wait()


def fused_on_device(
    tokens,
    segment_ids,
    norm_gain,
    w_mamba_in,
    w_ssm_param,
    ssm_rate,
    dt_bias,
    skip_gain,
    ssm_norm_gain,
    w_mamba_out,
    w_qkv,
    w_attn_out,
):
    n = lax.axis_size("ctx")
    chips = n // 2
    rows, model = tokens.shape[1:]
    width = w_mamba_in.shape[2]
    length = n * rows
    heads = ssm_rate.shape[1]
    segments = jnp.broadcast_to(segment_ids.astype(float32), (8, rows))
    small = jnp.concatenate([ssm_rate, dt_bias, skip_gain], axis=0).astype(float32)
    small = jnp.concatenate([small, jnp.zeros((5, heads), float32)], axis=0)
    dma = pltpu.SemaphoreType.DMA
    vmem = pl.BlockSpec(memory_space=pltpu.VMEM)
    result = pl.pallas_call(
        fused_kernel,
        out_shape=jax.ShapeDtypeStruct((rows, model), bfloat16),
        in_specs=[vmem] * 10,
        out_specs=vmem,
        scratch_shapes=[
            pltpu.VMEM((rows, model), bfloat16),
            pltpu.VMEM((n, 8, rows), float32),
            pltpu.VMEM((length, rows), float32),
            pltpu.VMEM((8, length), float32),
            pltpu.VMEM((8, rows), float32),
            pltpu.VMEM((STATE, width), float32),
            pltpu.VMEM((n, rows, model), bfloat16),
            pltpu.VMEM((n, rows, model), bfloat16),
            pltpu.VMEM((2, rows, width), bfloat16),
            pltpu.VMEM((2, rows, ATTN_DIM), bfloat16),
            pltpu.VMEM((3, model, ATTN_DIM), bfloat16),
            pltpu.VMEM((rows, model), bfloat16),
            pltpu.VMEM((length, ATTN_DIM), bfloat16),
            pltpu.VMEM((length, ATTN_DIM), bfloat16),
            pltpu.VMEM((rows, model), float32),
            pltpu.VMEM((rows, model), float32),
            pltpu.VMEM((n, 8, rows), float32),
            pltpu.VMEM((n, 8, rows), float32),
            pltpu.VMEM((2, chips, rows, model), bfloat16),
            pltpu.VMEM((2, chips, rows, model), bfloat16),
            pltpu.VMEM((2, chips, rows, model), bfloat16),
            pltpu.VMEM((2, chips, rows, model), bfloat16),
            dma((5,)),
            dma((n,)),
            dma((n,)),
            dma((2, chips)),
            dma((2, chips)),
            dma((2, n)),
            dma((3, n)),
            dma((1,)),
            dma((3,)),
            dma((n,)),
            dma((n,)),
            dma((2, chips)),
            dma((2, chips)),
            dma((2, chips)),
            dma((2, chips)),
        ],
        compiler_params=pltpu.CompilerParams(
            collective_id=0, has_side_effects=True, vmem_limit_bytes=48 * 1024 * 1024
        ),
    )(
        tokens[0],
        segments,
        norm_gain[0],
        w_mamba_in[0],
        w_ssm_param[0],
        small,
        ssm_norm_gain,
        w_mamba_out[0],
        w_qkv[0],
        w_attn_out[0],
    )
    return result[None]


def on_device(
    tokens,
    segment_ids,
    norm_gain,
    w_mamba_in,
    w_ssm_param,
    ssm_rate,
    dt_bias,
    skip_gain,
    ssm_norm_gain,
    w_mamba_out,
    w_qkv,
    w_attn_out,
):
    if fits_fused(tokens, w_qkv):
        return fused_on_device(
            tokens,
            segment_ids,
            norm_gain,
            w_mamba_in,
            w_ssm_param,
            ssm_rate,
            dt_bias,
            skip_gain,
            ssm_norm_gain,
            w_mamba_out,
            w_qkv,
            w_attn_out,
        )
    arrived = from_behind(
        (
            norm_gain,
            w_mamba_in,
            w_ssm_param,
            ssm_rate,
            dt_bias,
            skip_gain,
            ssm_norm_gain,
            w_mamba_out,
            w_qkv,
            w_attn_out,
        ),
        "blk",
        1,
    )
    section = tuple((item[0] for item in arrived))
    result = layer_pair(tokens[0], segment_ids[0], section)
    return result[None]


def solution(mesh):
    return jax.shard_map(
        on_device,
        mesh=mesh,
        in_specs=(
            P("blk", "ctx", None),
            P("blk", "ctx"),
            P("blk", None, None),
            P("blk", None, "ctx"),
            P("blk", None, None),
            P("blk", None),
            P("blk", None),
            P("blk", None),
            P("blk", None),
            P("blk", "ctx", None),
            P("blk", None, "ctx"),
            P("blk", "ctx", None),
        ),
        out_specs=P("blk", "ctx", None),
        check_vma=False,
    )
```

```python
import functools
import math

import jax
import jax.numpy as jnp
from jax import lax
from jax.experimental import pallas as pl
from jax.experimental.pallas import tpu as pltpu
from jax.sharding import PartitionSpec as P

INNER = 2048
HEAD_DIM = 64
STATE = 64
QUERY_HEADS = 8
KV_HEADS = 4
ATTN_DIM = 128
SPAN = 64


epsilon = 1e-05
highest = lax.Precision.HIGHEST


def prefix(value, axis, join, neutral):
    count, mine = (lax.axis_size(axis), lax.axis_index(axis))
    pieces = jax.tree.map(lambda part: lax.all_gather(part, axis), value)
    so_far = jax.tree.map(
        lambda part, zero: jnp.full_like(part, 0) + jnp.asarray(zero, part.dtype), value, neutral
    )

    def hop(position, so_far):
        longer = join(so_far, jax.tree.map(lambda part: part[position], pieces))
        return jax.tree.map(lambda new, old: jnp.where(position < mine, new, old), longer, so_far)

    return lax.fori_loop(0, count - 1, hop, so_far)


def from_behind(value, axis, steps):
    count = lax.axis_size(axis)
    pairs = [(source, (source + steps) % count) for source in range(count)]
    return lax.ppermute(value, axis, pairs)


def rms_norm(values, gain):
    values = values.astype(jnp.float32)
    scale = lax.rsqrt(jnp.mean(values * values, axis=-1, keepdims=True) + epsilon)
    return values * scale * gain.astype(jnp.float32)


def running_sum(values):
    count = values.shape[0]
    lower = jnp.tril(jnp.ones((count, count), jnp.float32))
    return jnp.dot(lower, values, precision=highest)


def span_update(carry, block):
    state, prev_segment = carry
    inner_value, bin_value, cout_value, delta, log_decay, segment = block
    cumul = running_sum(log_decay)
    order = jnp.arange(segment.shape[0])
    allowed = (order[:, None] >= order[None, :]) & (segment[:, None] == segment[None, :])
    differ = cumul[:, None, :] - cumul[None, :, :]
    factor = jnp.where(allowed[:, :, None], jnp.exp(jnp.minimum(differ, 0.0)), 0.0)
    intersection = jnp.dot(cout_value, bin_value.T, precision=highest)
    mixing = factor * intersection[:, :, None] * delta[None, :, :]
    within = jnp.einsum("tsh,shp->thp", mixing, inner_value, precision=highest)
    carried = jnp.where((segment == prev_segment)[:, None], jnp.exp(cumul), 0.0)
    across = jnp.einsum("tn,hpn->thp", cout_value, state, precision=highest) * carried[:, :, None]
    last_segment = segment[-1]
    keeping = (
        jnp.where((segment == last_segment)[:, None], jnp.exp(cumul[-1][None, :] - cumul), 0.0)
        * delta
    )
    fresh = jnp.einsum("sh,shp,sn->hpn", keeping, inner_value, bin_value, precision=highest)
    passing = jnp.where(prev_segment == last_segment, jnp.exp(cumul[-1]), 0.0)
    state = passing[:, None, None] * state + fresh
    return ((state, last_segment), within + across)


def combine_states(earlier, later):
    early_first, early_last, early_pass, early_state = earlier
    late_first, late_last, late_pass, late_state = later
    joined = (late_first == early_last) | (early_last < 0) | (late_first < 0)
    factor = jnp.where(joined, late_pass, 0.0)
    first = jnp.where(early_first < 0, late_first, early_first)
    last = jnp.where(late_last < 0, early_last, late_last)
    return (first, last, early_pass * factor, factor[:, None, None] * early_state + late_state)


def layer_pair(tokens, segment, weights):
    (
        norm_gain,
        w_mamba_in,
        w_ssm_param,
        ssm_rate,
        dt_bias,
        skip_gain,
        ssm_norm_gain,
        w_mamba_out,
        w_qkv,
        w_attn_out,
    ) = weights
    rows = tokens.shape[0]
    heads = ssm_rate.shape[0]
    offset = lax.axis_index("ctx") * rows
    normed = rms_norm(tokens, norm_gain[0]).astype(jnp.bfloat16)
    slab = jnp.dot(
        lax.all_gather(normed, "ctx", axis=0, tiled=True),
        w_mamba_in,
        preferred_element_type=jnp.float32,
    ).astype(jnp.bfloat16)
    inner = lax.all_to_all(slab, "ctx", split_axis=0, concat_axis=1, tiled=True)
    params = jnp.dot(normed, w_ssm_param, preferred_element_type=jnp.float32)
    bin_value = params[:, :STATE]
    cout_value = params[:, STATE : 2 * STATE]
    delta = jax.nn.softplus(params[:, 2 * STATE :] + dt_bias.astype(jnp.float32))
    log_decay = -delta * ssm_rate.astype(jnp.float32)
    inner_value = inner.astype(jnp.float32).reshape(rows, heads, HEAD_DIM)
    blocks = tuple(
        (
            item.reshape((rows // SPAN, SPAN) + item.shape[1:])
            for item in (inner_value, bin_value, cout_value, delta, log_decay, segment)
        )
    )
    start_carry = (jnp.zeros((heads, HEAD_DIM, STATE), jnp.float32), segment[0])
    (local_state, ignored), mixed = lax.scan(span_update, start_carry, blocks)
    device_decay = running_sum(log_decay)
    through = jnp.where(segment[0] == segment[-1], jnp.exp(device_decay[-1]), 0.0)
    element = (segment[0], segment[-1], through, local_state)
    identity = (
        jnp.array(-1, jnp.int32),
        jnp.array(-1, jnp.int32),
        jnp.ones_like(through),
        jnp.zeros_like(local_state),
    )
    scanned = prefix(element, "ctx", combine_states, identity)
    incoming_segment = scanned[1]
    incoming_state = scanned[3]
    linked = jnp.where((segment == incoming_segment)[:, None], jnp.exp(device_decay), 0.0)
    entering = (
        jnp.einsum("tn,hpn->thp", cout_value, incoming_state, precision=highest)
        * linked[:, :, None]
    )
    mixed = (
        mixed.reshape(rows, heads, HEAD_DIM)
        + entering
        + skip_gain.astype(jnp.float32)[None, :, None] * inner_value
    )
    ssm_out = rms_norm(mixed.reshape(rows, INNER), ssm_norm_gain).astype(jnp.bfloat16)
    columns = ssm_out
    first = tokens.astype(jnp.float32) + jnp.dot(
        columns,
        lax.all_gather(w_mamba_out, "ctx", axis=0, tiled=True),
        preferred_element_type=jnp.float32,
    )
    hidden = rms_norm(first, norm_gain[1]).astype(jnp.bfloat16)
    projected = jnp.dot(
        hidden, lax.all_gather(w_qkv, "ctx", axis=1, tiled=True), preferred_element_type=jnp.float32
    ).astype(jnp.bfloat16)
    groups = QUERY_HEADS // KV_HEADS
    query = projected[:, : QUERY_HEADS * ATTN_DIM].reshape(rows, KV_HEADS, groups, ATTN_DIM)
    keys = projected[:, QUERY_HEADS * ATTN_DIM : (QUERY_HEADS + KV_HEADS) * ATTN_DIM]
    values = projected[:, (QUERY_HEADS + KV_HEADS) * ATTN_DIM :]
    positions = offset + jnp.arange(rows)
    scale = 1.0 / math.sqrt(ATTN_DIM)
    top = jnp.full((KV_HEADS, groups, rows), -1e30, jnp.float32)
    key_piece = lax.all_gather(keys, "ctx", axis=0, tiled=True)
    value_piece = lax.all_gather(values, "ctx", axis=0, tiled=True)
    segment_piece = lax.all_gather(segment, "ctx", axis=0, tiled=True)
    count = key_piece.shape[0]
    key_position = jnp.arange(count)
    scores = (
        jnp.einsum(
            "tkgd,skd->kgts",
            query,
            key_piece.reshape(count, KV_HEADS, ATTN_DIM),
            preferred_element_type=jnp.float32,
        )
        * scale
    )
    allowed = (key_position[None, :] <= positions[:, None]) & (
        segment_piece[None, :] == segment[:, None]
    )
    scores = jnp.where(allowed, scores, -1e30)
    new_top = jnp.maximum(top, jnp.max(scores, axis=-1))
    probs = jnp.where(allowed, jnp.exp(scores - new_top[..., None]), 0.0)
    total = jnp.sum(probs, axis=-1)
    attend_context = jnp.einsum(
        "kgts,skd->kgtd",
        probs.astype(jnp.bfloat16),
        value_piece.reshape(count, KV_HEADS, ATTN_DIM),
        preferred_element_type=jnp.float32,
    )
    top, total, context = (new_top, total, attend_context)
    context = context / total[..., None]
    context = (
        jnp.transpose(context, (2, 0, 1, 3))
        .reshape(rows, QUERY_HEADS * ATTN_DIM)
        .astype(jnp.bfloat16)
    )
    columns = context
    result = first + jnp.dot(
        columns,
        lax.all_gather(w_attn_out, "ctx", axis=0, tiled=True),
        preferred_element_type=jnp.float32,
    )
    return result.astype(jnp.bfloat16)


MESH = pl.DeviceIdType.MESH
float32, bfloat16 = jnp.float32, jnp.bfloat16


def fits_fused(tokens, w_qkv):
    count = lax.axis_size("ctx")
    return (
        lax.axis_size("blk") > 1
        and count == QUERY_HEADS
        and QUERY_HEADS == 2 * KV_HEADS
        and tokens.shape[1] % 128 == 0
        and w_qkv.shape[2] % ATTN_DIM == 0
    )


def remote(source, target, send_sem, recv_sem, blk, ctx):
    return pltpu.make_async_remote_copy(
        src_ref=source,
        dst_ref=target,
        send_sem=send_sem,
        recv_sem=recv_sem,
        device_id=(blk, ctx),
        device_id_type=MESH,
    )


def dot(a, b, contract=((1,), (0,)), precision=None):
    return lax.dot_general(
        a, b, (contract, ((), ())), precision=precision, preferred_element_type=float32
    )


def halves(value):
    high = value.astype(bfloat16)
    return high, (value - high.astype(float32)).astype(bfloat16)


def to_column(row, rows):
    return jnp.broadcast_to(row, (rows, rows)).T


def fused_kernel(
    tok_ref,
    seg_ref,
    gain_ref,
    win_ref,
    wssm_ref,
    small_ref,
    sgain_ref,
    wout_ref,
    wqkv_ref,
    wao_ref,
    out_ref,
    xbuf,
    segbuf,
    segcol,
    segrow,
    prev_ref,
    state_ref,
    nall,
    hall,
    mix_ref,
    csend,
    cbuf,
    wao_all,
    wbuf,
    qbuf,
    kbuf,
    vbuf,
    own_ref,
    first_ref,
    sqsend,
    sqbuf,
    pairsend,
    pairbuf,
    rssend,
    rsbuf,
    hop_sem,
    hop_out,
    hop_in,
    seg_send,
    seg_recv,
    c_send,
    c_recv,
    relay_sem,
    w_send,
    w_fwd,
    w_recv,
    sq_send,
    sq_recv,
    pair_send,
    pair_recv,
    rs_send,
    rs_recv,
):
    n, nb = lax.axis_size("ctx"), lax.axis_size("blk")
    chips = n // 2
    me, blk = lax.axis_index("ctx"), lax.axis_index("blk")
    chip, core = me // 2, me % 2
    sibling = chip * 2 + 1 - core
    ahead, behind = (blk + 1) % nb, (blk + nb - 1) % nb
    rows, model = tok_ref.shape
    length = n * rows
    wide = 2 * rows
    width = win_ref.shape[1]
    heads = small_ref.shape[1]
    mine = width // HEAD_DIM
    inner_total = sgain_ref.shape[1]
    held = wqkv_ref.shape[1] // ATTN_DIM

    barrier = pltpu.get_barrier_semaphore()
    for k in range(1, n):
        pl.semaphore_signal(barrier, inc=1, device_id=(blk, (me + k) % n), device_id_type=MESH)
    for other in (ahead, behind):
        pl.semaphore_signal(barrier, inc=1, device_id=(other, me), device_id_type=MESH)
    pl.semaphore_wait(barrier, n + 1)

    parts = 4 if rows % 64 == 0 else 1

    def hop_copy(q):
        here = pl.ds(q * (rows // parts), rows // parts)
        return remote(
            tok_ref.at[here], xbuf.at[here], hop_out.at[q], hop_in.at[q], behind, me
        )

    for q in range(parts):
        hop_copy(q).start()
    seg_hop = remote(seg_ref, segbuf.at[me], hop_sem.at[2], seg_recv.at[me], behind, me)
    seg_hop.start()

    def passing(way, buf, stage, pieces, block, q):
        height = buf.shape[1] // pieces
        part = buf.at[block, pl.ds(q * height, height)]
        target = (me + 2) % n if way == 0 else (me + n - 2) % n if way == 1 else sibling
        return remote(
            part, part, relay_sem.at[stage, way, block, q], relay_sem.at[stage, 3, block, q], blk, target
        )

    def each_way(right, left, act):
        if right:
            pl.when(chip < chips - 1)(lambda: act(0))
        if left:
            pl.when(chip > 0)(lambda: act(1))
        act(2)

    def relay_pass(buf, stage, pieces, block, q, right, left):
        each_way(right, left, lambda way: passing(way, buf, stage, pieces, block, q).start())

    def relay_wait(buf, stage, pieces, block, q):
        passing(2, buf, stage, pieces, block, q).wait_recv()

    def relay_round(buf, stage, pieces, k):
        for q in range(pieces):

            @pl.when(chip >= k)
            def _():
                relay_wait(buf, stage, pieces, me - 2 * k, q)
                relay_pass(buf, stage, pieces, me - 2 * k, q, True, False)

            @pl.when(chip + k < chips)
            def _():
                relay_wait(buf, stage, pieces, me + 2 * k, q)
                relay_pass(buf, stage, pieces, me + 2 * k, q, False, True)

    def relay_last(buf, stage, pieces, p):
        for q in range(pieces):
            relay_wait(buf, stage, pieces, 2 * p + 1 - core, q)

    def relay_close(buf, stage, pieces):
        for q in range(pieces):
            for k in range(chips):
                for right, left in ((True, True),) if k == 0 else ((True, False), (False, True)):
                    block = me - 2 * k if right else me + 2 * k
                    here = chip >= k if right else chip + k < chips

                    @pl.when(here)
                    def _():
                        each_way(
                            right,
                            left,
                            lambda way: passing(way, buf, stage, pieces, block, q).wait_send(),
                        )

    wao_all[me] = wao_ref[...]
    relay_pass(wao_all, 2, 1, me, 0, True, True)

    plan = []
    for e in range(n):
        plan.append((0, e, e))
    for j in range(KV_HEADS):
        plan.append((1, QUERY_HEADS + j, 2 * j))
        plan.append((2, QUERY_HEADS + KV_HEADS + j, 2 * j + 1))

    def weight_copy(kind, head, target):
        part = wqkv_ref.at[:, pl.ds((head % held) * ATTN_DIM, ATTN_DIM)]
        return remote(part, wbuf.at[kind], w_send.at[kind, target], w_recv.at[kind], blk, target)

    for kind, head, target in plan:

        @pl.when(me == head // held)
        def _():
            if head // held == target:
                wbuf[kind] = wqkv_ref[:, (head % held) * ATTN_DIM : (head % held + 1) * ATTN_DIM]
            else:
                weight_copy(kind, head, target).start()

    def weight_wait(kind):
        remote(wbuf.at[0], wbuf.at[kind], w_send.at[0, 0], w_recv.at[kind], blk, sibling).wait_recv()

    def not_own(kind, then):
        own = [t for k, h, t in plan if k == kind and h // held == t]
        here = me >= 0
        for target in own:
            here = here & (me != target)
        pl.when(here)(then)

    def pair_copy(stage, p):
        return remote(
            pairsend.at[stage, p],
            pairbuf.at[stage, p],
            pair_send.at[stage, p],
            pair_recv.at[stage, p],
            blk,
            sibling,
        )

    def rs_copy(stage, p, source):
        return remote(
            rssend.at[stage, p],
            rsbuf.at[stage, source],
            rs_send.at[stage, p],
            rs_recv.at[stage, source],
            blk,
            2 * p + core,
        )

    def scatter_step(stage, p, left, weight_ref):
        pairsend[stage, p] = dot(left[1 - core], weight_ref[...]).astype(bfloat16)
        pair_copy(stage, p).start()
        part = dot(left[core], weight_ref[...])
        pair_copy(stage, p).wait_recv()
        part = part + pairbuf[stage, p].astype(float32)

        @pl.when(p == chip)
        def _():
            own_ref[...] = part

        @pl.when(p != chip)
        def _():
            rssend[stage, p] = part.astype(bfloat16)
            rs_copy(stage, p, chip).start()

    def scatter_end(stage):
        total = own_ref[...]
        for k in range(1, chips):
            source = (chip + k) % chips
            rs_copy(stage, source, source).wait_recv()
            total = total + rsbuf[stage, source].astype(float32)
        return total

    def sq_copy(target, source):
        return remote(
            sqsend.at[target], sqbuf.at[source], sq_send.at[target], sq_recv.at[source], blk, target
        )

    def context_copy(target, source):
        return remote(
            csend.at[target], cbuf.at[source], c_send.at[target], c_recv.at[source], blk, target
        )

    for q in range(parts):
        here = slice(q * (rows // parts), (q + 1) * (rows // parts))
        hop_copy(q).wait_recv()
        x = xbuf[here, :].astype(float32)
        scale = lax.rsqrt(jnp.mean(x * x, axis=-1, keepdims=True) + epsilon)
        nall[me, here, :] = (x * scale * gain_ref[0:1, :].astype(float32)).astype(bfloat16)
        relay_pass(nall, 0, parts, me, q, True, True)
    sends = []
    seg_hop_in = remote(seg_ref, segbuf.at[me], hop_sem.at[2], seg_recv.at[me], behind, me)
    seg_hop_in.wait_recv()
    for k in range(1, n):
        copy = remote(
            segbuf.at[me], segbuf.at[me], seg_send.at[k], seg_recv.at[me], blk, (me + k) % n
        )
        copy.start()
        sends.append(copy)
    for k in range(1, n):
        source = (me + k) % n
        remote(
            segbuf.at[source], segbuf.at[source], seg_send.at[k], seg_recv.at[source], blk, source
        ).wait_recv()
    for k in range(1, chips):
        relay_round(nall, 0, parts, k)
    relay_round(wao_all, 2, 1, 1)
    for j in range(n):
        segrow[:, j * rows : (j + 1) * rows] = segbuf[j]
        segcol[j * rows : (j + 1) * rows, :] = to_column(segbuf[j][0:1, :], rows)
    prev_ref[...] = segbuf[0]
    state_ref[...] = jnp.zeros_like(state_ref)

    head_row = lax.broadcasted_iota(jnp.int32, (heads, 128), 0)
    head_lane = lax.broadcasted_iota(jnp.int32, (heads, 128), 1)
    pick = (head_row == head_lane + me * mine).astype(float32)
    pick = jnp.where(head_lane < mine, pick, 0.0)
    wide_row = lax.broadcasted_iota(jnp.int32, (heads, width), 0)
    wide_lane = lax.broadcasted_iota(jnp.int32, (heads, width), 1)
    spread = (wide_row == wide_lane // HEAD_DIM + me * mine).astype(float32)
    lane_head = lax.broadcasted_iota(jnp.int32, (wide, width), 1) // HEAD_DIM
    later = lax.broadcasted_iota(jnp.int32, (wide, wide), 0)
    earlier = lax.broadcasted_iota(jnp.int32, (wide, wide), 1)
    lower = (later >= earlier).astype(float32)
    rate, bias = small_ref[0:1, :], small_ref[1:2, :]
    skip = dot(small_ref[...], spread, precision=highest)[2:3, :]
    sgain = sgain_ref[:, pl.ds(pl.multiple_of(me * width, width), width)].astype(float32)

    def mamba_step(p, carry):
        relay_last(nall, 0, parts, p)
        block = nall[pl.ds(2 * p, 2)].reshape(wide, model)
        u = dot(block, win_ref[...]).astype(bfloat16).astype(float32)
        params = dot(block, wssm_ref[...])
        bin_value = params[:, :STATE]
        cout_value = params[:, STATE : 2 * STATE]
        raw = params[:, 2 * STATE :] + bias
        delta = jnp.maximum(raw, 0.0) + jnp.log1p(jnp.exp(-jnp.abs(raw)))
        cumul = dot(lower, -delta * rate, precision=highest)
        cumul_column = dot(cumul, pick, precision=highest)
        cumul_row = cumul_column.T
        cumul_wide = dot(cumul, spread, precision=highest)
        fed = dot(delta, spread, precision=highest) * u
        fed_high, fed_low = halves(fed)
        own = jnp.sum(bin_value * cout_value, axis=-1, keepdims=True)
        begin = pl.multiple_of(p * wide, wide)
        seg_column = segcol[pl.ds(begin, wide), 0:1]
        seg_row = segrow[0:1, pl.ds(begin, wide)]
        prev = prev_ref[0:1, 0:1]
        last = seg_row[0:1, wide - 1 : wide]
        allowed = (seg_column == seg_row) & (later > earlier)
        crossing = dot(cout_value, bin_value, ((1,), (1,)), precision=highest)
        mixed = jnp.zeros((wide, width), float32)
        for h in range(mine):
            differ = cumul_column[:, h : h + 1] - cumul_row[h : h + 1, :]
            factor = jnp.where(allowed, jnp.exp(jnp.minimum(differ, 0.0)) * crossing, 0.0)
            high, low = halves(factor)
            within = dot(high, fed_high) + (dot(low, fed_high) + dot(high, fed_low))
            mixed = jnp.where(lane_head == h, within, mixed)
        state = state_ref[...]
        mixed = mixed + dot(cout_value, state, precision=highest) * jnp.where(
            seg_column == prev, jnp.exp(cumul_wide), 0.0
        )
        mixed = mixed + (own * fed + skip * u)
        final = cumul_wide[wide - 1 : wide, :]
        keep = jnp.where(seg_column == last, jnp.exp(final - cumul_wide), 0.0)
        fresh = dot(bin_value, keep * fed, ((0,), (0,)), precision=highest)
        state_ref[...] = jnp.where(prev == last, jnp.exp(final), 0.0) * state + fresh
        prev_ref[...] = jnp.broadcast_to(last, prev_ref.shape)
        square = jnp.sum(mixed * mixed, axis=-1, keepdims=True)
        mixed = (mixed * sgain).astype(bfloat16)
        for o in range(2):
            mix_ref[o] = mixed[o * rows : (o + 1) * rows]
            flat = jnp.broadcast_to(square[o * rows : (o + 1) * rows], (rows, rows)).T[:8]
            target = 2 * p + o

            @pl.when(target == me)
            def _():
                sqbuf[me] = flat

            @pl.when(target != me)
            def _():
                sqsend[target] = flat
                sq_copy(target, me).start()

        scatter_step(0, p, mix_ref, wout_ref)
        return carry

    lax.fori_loop(0, chips, mamba_step, 0)

    not_own(1, lambda: pl.when(core == 0)(lambda: weight_wait(1)))
    not_own(2, lambda: pl.when(core == 1)(lambda: weight_wait(2)))
    passed = remote(
        wbuf.at[1 + core], wbuf.at[1 + core], w_fwd.at[0], w_recv.at[1 + core], blk, sibling
    )
    passed.start()
    sends.append(passed)

    relay_round(wao_all, 2, 1, 2)
    total = scatter_end(0)
    for k in range(1, n):
        source = (me + k) % n
        sq_copy(source, source).wait_recv()
    squares = sqbuf[0]
    for j in range(1, n):
        squares = squares + sqbuf[j]
    squares = to_column(squares[0:1, :], rows)[:, 0:1]
    first = xbuf[...].astype(float32) + total * lax.rsqrt(squares / inner_total + epsilon)
    first_ref[...] = first
    scale = lax.rsqrt(jnp.mean(first * first, axis=-1, keepdims=True) + epsilon)
    hall[me] = (first * scale * gain_ref[1:2, :].astype(float32)).astype(bfloat16)
    for q in range(2):
        relay_pass(hall, 1, 2, me, q, True, True)
    for k in range(1, chips):
        relay_round(hall, 1, 2, k)
    relay_round(wao_all, 2, 1, 3)

    not_own(0, lambda: weight_wait(0))
    weight_wait(2 - core)
    for p in range(chips):
        relay_last(hall, 1, 2, p)
        block = hall[pl.ds(2 * p, 2)].reshape(wide, model)
        here = slice(p * wide, (p + 1) * wide)
        upto = (p + 1) * wide
        query = dot(block, wbuf[0]).astype(bfloat16)
        kbuf[here, :] = dot(block, wbuf[1]).astype(bfloat16)
        vbuf[here, :] = dot(block, wbuf[2]).astype(bfloat16)
        scores = dot(query, kbuf[:upto, :], ((1,), (1,))) * (1.0 / math.sqrt(ATTN_DIM))
        at = p * wide + lax.broadcasted_iota(jnp.int32, (wide, upto), 0)
        key_at = lax.broadcasted_iota(jnp.int32, (wide, upto), 1)
        allowed = (key_at <= at) & (segcol[here, 0:1] == segrow[0:1, :upto])
        scores = jnp.where(allowed, scores, -1e30)
        top = jnp.max(scores, axis=-1, keepdims=True)
        probs = jnp.where(allowed, jnp.exp(scores - top), 0.0)
        weight = jnp.sum(probs, axis=-1, keepdims=True)
        context = (dot(probs.astype(bfloat16), vbuf[:upto, :]) / weight).astype(bfloat16)
        for o in range(2):
            target = 2 * p + o
            part = context[o * rows : (o + 1) * rows]

            @pl.when(target == me)
            def _():
                cbuf[me] = part

            @pl.when(target != me)
            def _():
                csend[target] = part
                context_copy(target, me).start()

    for p in range(chips):
        relay_last(wao_all, 2, 1, p)
    for k in range(1, n):
        source = (me + k) % n
        context_copy(source, source).wait_recv()
    context = jnp.concatenate([cbuf[j] for j in range(n)], axis=1)
    result = first_ref[...] + dot(context, wao_all[...].reshape(n * ATTN_DIM, model))
    qbuf[...] = result.astype(bfloat16)
    back = remote(qbuf, out_ref, hop_sem.at[3], hop_sem.at[4], ahead, me)
    back.start()

    for copy in sends:
        copy.wait_send()
    for q in range(parts):
        hop_copy(q).wait_send()
    relay_close(nall, 0, parts)
    relay_close(hall, 1, 2)
    relay_close(wao_all, 2, 1)
    seg_hop.wait_send()
    for kind, head, target in plan:
        if head // held != target:

            @pl.when(me == head // held)
            def _():
                weight_copy(kind, head, target).wait_send()

    for j in range(n):

        @pl.when(me != j)
        def _():
            sq_copy(j, me).wait_send()
            context_copy(j, me).wait_send()

    for p in range(chips):
        pair_copy(0, p).wait_send()

        @pl.when(chip != p)
        def _():
            rs_copy(0, p, chip).wait_send()

    back.wait()


def fused_on_device(
    tokens,
    segment_ids,
    norm_gain,
    w_mamba_in,
    w_ssm_param,
    ssm_rate,
    dt_bias,
    skip_gain,
    ssm_norm_gain,
    w_mamba_out,
    w_qkv,
    w_attn_out,
):
    n = lax.axis_size("ctx")
    chips = n // 2
    rows, model = tokens.shape[1:]
    width = w_mamba_in.shape[2]
    length = n * rows
    heads = ssm_rate.shape[1]
    segments = jnp.broadcast_to(segment_ids.astype(float32), (8, rows))
    small = jnp.concatenate([ssm_rate, dt_bias, skip_gain], axis=0).astype(float32)
    small = jnp.concatenate([small, jnp.zeros((5, heads), float32)], axis=0)
    dma = pltpu.SemaphoreType.DMA
    vmem = pl.BlockSpec(memory_space=pltpu.VMEM)
    result = pl.pallas_call(
        fused_kernel,
        out_shape=jax.ShapeDtypeStruct((rows, model), bfloat16),
        in_specs=[vmem] * 10,
        out_specs=vmem,
        scratch_shapes=[
            pltpu.VMEM((rows, model), bfloat16),
            pltpu.VMEM((n, 8, rows), float32),
            pltpu.VMEM((length, rows), float32),
            pltpu.VMEM((8, length), float32),
            pltpu.VMEM((8, rows), float32),
            pltpu.VMEM((STATE, width), float32),
            pltpu.VMEM((n, rows, model), bfloat16),
            pltpu.VMEM((n, rows, model), bfloat16),
            pltpu.VMEM((2, rows, width), bfloat16),
            pltpu.VMEM((n, rows, ATTN_DIM), bfloat16),
            pltpu.VMEM((n, rows, ATTN_DIM), bfloat16),
            pltpu.VMEM((n, ATTN_DIM, model), bfloat16),
            pltpu.VMEM((3, model, ATTN_DIM), bfloat16),
            pltpu.VMEM((rows, model), bfloat16),
            pltpu.VMEM((length, ATTN_DIM), bfloat16),
            pltpu.VMEM((length, ATTN_DIM), bfloat16),
            pltpu.VMEM((rows, model), float32),
            pltpu.VMEM((rows, model), float32),
            pltpu.VMEM((n, 8, rows), float32),
            pltpu.VMEM((n, 8, rows), float32),
            pltpu.VMEM((1, chips, rows, model), bfloat16),
            pltpu.VMEM((1, chips, rows, model), bfloat16),
            pltpu.VMEM((1, chips, rows, model), bfloat16),
            pltpu.VMEM((1, chips, rows, model), bfloat16),
            dma((5,)),
            dma((4,)),
            dma((4,)),
            dma((n,)),
            dma((n,)),
            dma((n,)),
            dma((n,)),
            dma((3, 4, n, 4)),
            dma((3, n)),
            dma((1,)),
            dma((3,)),
            dma((n,)),
            dma((n,)),
            dma((2, chips)),
            dma((2, chips)),
            dma((2, chips)),
            dma((2, chips)),
        ],
        compiler_params=pltpu.CompilerParams(
            collective_id=0, has_side_effects=True, vmem_limit_bytes=48 * 1024 * 1024
        ),
    )(
        tokens[0],
        segments,
        norm_gain[0],
        w_mamba_in[0],
        w_ssm_param[0],
        small,
        ssm_norm_gain,
        w_mamba_out[0],
        w_qkv[0],
        w_attn_out[0],
    )
    return result[None]


def on_device(
    tokens,
    segment_ids,
    norm_gain,
    w_mamba_in,
    w_ssm_param,
    ssm_rate,
    dt_bias,
    skip_gain,
    ssm_norm_gain,
    w_mamba_out,
    w_qkv,
    w_attn_out,
):
    if fits_fused(tokens, w_qkv):
        return fused_on_device(
            tokens,
            segment_ids,
            norm_gain,
            w_mamba_in,
            w_ssm_param,
            ssm_rate,
            dt_bias,
            skip_gain,
            ssm_norm_gain,
            w_mamba_out,
            w_qkv,
            w_attn_out,
        )
    arrived = from_behind(
        (
            norm_gain,
            w_mamba_in,
            w_ssm_param,
            ssm_rate,
            dt_bias,
            skip_gain,
            ssm_norm_gain,
            w_mamba_out,
            w_qkv,
            w_attn_out,
        ),
        "blk",
        1,
    )
    section = tuple((item[0] for item in arrived))
    result = layer_pair(tokens[0], segment_ids[0], section)
    return result[None]


def solution(mesh):
    return jax.shard_map(
        on_device,
        mesh=mesh,
        in_specs=(
            P("blk", "ctx", None),
            P("blk", "ctx"),
            P("blk", None, None),
            P("blk", None, "ctx"),
            P("blk", None, None),
            P("blk", None),
            P("blk", None),
            P("blk", None),
            P("blk", None),
            P("blk", "ctx", None),
            P("blk", None, "ctx"),
            P("blk", "ctx", None),
        ),
        out_specs=P("blk", "ctx", None),
        check_vma=False,
    )
```
